32 devices in a mesh: segment: 2 (over core), inline: 4 (over z), xline: 4 (over y, x).
Axes of the slice: x: 2, y: 2, z: 4, core: 2. Of those that a mesh axis runs over, the one named last changes fastest.
Arguments:
- survey: float32 [2, 16, 16, 1024], P(None, 'inline', 'xline'), may hold values from -6 to 6
- conduct: bfloat16 [3, 2, 16, 16, 1024], P(None, None, 'inline', 'xline'), may hold values from 0.099609375 to 1
- widths: int32 [2, 4], P(None, 'inline'), may hold values from 2 to 4, as said below
Outputs:
- coherence: float32 [2, 16, 16, 1024], P('segment', 'inline', 'xline')
- curvature: float32 [2, 16, 16, 1024], P('segment', 'inline', 'xline')
The draws below stay inside these ranges and needn't reach their ends.
Inputs may be any that keep to these rules, and one draw needn't show every extreme that they name: `widths`: in every micro-batch some device holds exactly 4 live rows and another exactly 2.
All inputs are finite; a program needn't handle non-finite values.
Results may differ from the reference program's by a relative error of at most 0.0003.
Values sent between devices are 32-bit elements; how exact they have to be, the bound alone decides.
A program may use at most 64 MiB of HBM per device.

```python
import math
import jax
import jax.numpy as jnp

SLAB = 4
NT = 1024
STEPS = 2
MB = 2
NI = 16
NX = 16
N_INLINE = 4


def draw_widths(key, part):
    first_key, second_key = jax.random.split(jax.random.fold_in(key, 11))
    values = jax.random.randint(first_key, (MB, N_INLINE), SLAB // 2, SLAB + 1)
    spot = jax.random.randint(second_key, (MB,), 0, N_INLINE)
    columns = jnp.arange(N_INLINE)[None, :]
    values = jnp.where(columns == spot[:, None], SLAB, values)
    values = jnp.where(columns == ((spot + 1) % N_INLINE)[:, None], SLAB // 2, values)
    return values.astype(jnp.int32)


def level_of(rng, extent, cuts, smallest, top_value):
    def one(axis_at, shards_of):
        heights = jax.random.uniform(jax.random.fold_in(jax.random.fold_in(rng, 6), axis_at), (shards_of,), jnp.float32, smallest / len(cuts), top_value / len(cuts))
        return jnp.repeat(jnp.exp(heights), extent[axis_at] // shards_of).reshape((-1,) + (1,) * (len(extent) - axis_at - 1))

    gain = one(*cuts[0])
    for cut in cuts[1:]:
        gain = gain * one(*cut)
    return gain


def centred(rng, shape, spread, limit, shards=(), kind=jnp.bfloat16):
    level = level_of(rng, shape, shards, -0.22, 0.18) if shards else 1.0
    values = jax.random.normal(rng, shape, jnp.float32) * spread * level
    return jnp.minimum(jnp.maximum(values, -limit), limit).astype(kind)


def setup_inputs(seed: int = 0) -> dict:
    streams_of = jax.random.split(jax.random.key(seed), 4)
    survey = centred(streams_of[0], (MB, NI, NX, NT), 1.0, 6.0, ((1, 4), (2, 4)), jnp.float32)
    conduct = jnp.clip(jnp.exp(math.log(1.0) - 2.306499 * jax.random.uniform(streams_of[1], (3, MB, NI, NX, NT), jnp.float32) ** level_of(streams_of[1], (3, MB, NI, NX, NT), ((2, 4), (3, 4)), -0.2, 0.2)), 0.099609375, 1.0).astype(jnp.bfloat16)
    widths = draw_widths(jax.random.fold_in(streams_of[3], 71), 0)
    return dict(survey=survey, conduct=conduct, widths=widths)


step_size = 0.15
epsilon = 1e-6


def links(width_row):
    rows_all = SLAB * N_INLINE
    cell = jnp.arange(rows_all, dtype=jnp.int32)
    device = cell // SLAB
    within = cell % SLAB
    width = width_row[device]
    later = jnp.where(within < width - 1, cell + 1, jnp.where(device < N_INLINE - 1, (device + 1) * SLAB, cell)).astype(jnp.int32)
    before_width = width_row[jnp.maximum(device - 1, 0)]
    earlier = jnp.where(within > 0, cell - 1, jnp.where(device > 0, (device - 1) * SLAB + before_width - 1, cell)).astype(jnp.int32)
    return later, earlier, within < width


def clamped(length):
    index = jnp.arange(length, dtype=jnp.int32)
    return jnp.minimum(index + 1, length - 1).astype(jnp.int32), jnp.maximum(index - 1, 0).astype(jnp.int32)


def single_batch(field, coeffs, width_row):
    later, earlier, live = links(width_row)
    pairs = [(later, earlier), clamped(NX), clamped(NT)]
    live_cells = live[:, None, None]
    values = jnp.where(live_cells, field, 0.0)
    for repeat in range(STEPS):
        change = jnp.zeros_like(values)
        for which_axis in range(3):
            kk = coeffs[which_axis]
            for index in pairs[which_axis]:
                change = change + 0.5 * (kk + jnp.take(kk, index, axis=which_axis)) * (jnp.take(values, index, axis=which_axis) - values)
        values = values + step_size * change
    smooth = values
    grads = []
    for which_axis in range(3):
        up_index, down_index = pairs[which_axis]
        grads.append(0.5 * (jnp.take(smooth, up_index, axis=which_axis) - jnp.take(smooth, down_index, axis=which_axis)))
    seconds = []
    for which_axis in range(2):
        up_index, down_index = pairs[which_axis]
        seconds.append(jnp.take(smooth, up_index, axis=which_axis) + jnp.take(smooth, down_index, axis=which_axis) - 2.0 * smooth)
    combos = [(0, 0), (1, 1), (2, 2), (0, 1), (0, 2), (1, 2)]
    tensor = []
    for first_index, second_index in combos:
        member = grads[first_index] * grads[second_index]
        for which_axis in range(3):
            up_index, down_index = pairs[which_axis]
            member = 0.25 * (jnp.take(member, up_index, axis=which_axis) + 2.0 * member + jnp.take(member, down_index, axis=which_axis))
        tensor.append(member)
    trace = tensor[0] + tensor[1] + tensor[2]
    minors = tensor[0] * tensor[1] - tensor[3] * tensor[3] + tensor[0] * tensor[2] - tensor[4] * tensor[4] + tensor[1] * tensor[2] - tensor[5] * tensor[5]
    coherence = 1.0 - 3.0 * minors / (trace * trace + epsilon)
    curvature = (seconds[0] + seconds[1]) / (1.0 + grads[0] * grads[0] + grads[1] * grads[1]) ** 1.5
    return jnp.where(live_cells, coherence, 0.0), jnp.where(live_cells, curvature, 0.0)


def reference(survey, conduct, widths):
    coherent_list = []
    curved_list = []
    for batch in range(MB):
        coeffs = conduct[:, batch].astype(jnp.float32)
        coherence, curvature = single_batch(survey[batch], coeffs, widths[batch])
        coherent_list.append(coherence)
        curved_list.append(curvature)
    return jnp.stack(coherent_list, 0), jnp.stack(curved_list, 0)
```

```python
import jax
import jax.numpy as jnp
from jax import lax
from jax.experimental import pallas as pl
from jax.experimental.pallas import tpu as pltpu
from jax.sharding import PartitionSpec as P

MESH = pl.DeviceIdType.MESH
step_size = 0.15
epsilon = 1e-06
half_step = 0.5 * step_size
SUB, LANE = 8, 128

LEFT, RIGHT, ABOVE, BELOW = (0, -1), (0, 1), (-1, 0), (1, 0)
DIRS = [LEFT, RIGHT, ABOVE, BELOW, (-1, -1), (-1, 1), (1, -1), (1, 1)]


def slots(side, corner):
    table, at = {}, 0
    for d in DIRS:
        n = corner if d[0] and d[1] else side
        table[d] = (at, n)
        at += n
    return table, at


FIRST, FIRST_LEN = slots(14, 3)
SECOND, SECOND_LEN = slots(8, 3)


def positions():
    lane = lax.broadcasted_iota(jnp.int32, (SUB, LANE), 1)
    sub = lax.broadcasted_iota(jnp.int32, (SUB, LANE), 0)
    return lane == 0, lane == LANE - 1, (lane == 0) & (sub == 0), (lane == LANE - 1) & (sub == SUB - 1)


def later(v, pos):
    n = v.ndim
    rolled = pltpu.roll(v, LANE - 1, n - 1)
    v_next = jnp.where(pos[1], pltpu.roll(rolled, SUB - 1, n - 2), rolled)
    return jnp.where(pos[3], v, v_next)


def around(v, pos):
    n = v.ndim
    rolled = pltpu.roll(v, 1, n - 1)
    return jnp.where(pos[0], pltpu.roll(rolled, 1, n - 2), rolled)


def earlier(v, pos):
    return jnp.where(pos[2], v, around(v, pos))


def pad_rows(value, before, after):
    zero = jnp.zeros((1,) + value.shape[1:], value.dtype)
    return jnp.concatenate([zero] * before + [value] + [zero] * after, 0)


def pad_cols(value, before, after):
    zero = jnp.zeros((value.shape[0], 1) + value.shape[2:], value.dtype)
    return jnp.concatenate([zero] * before + [value] + [zero] * after, 1)


def kernel(widths_ref, survey_ref, conduct_ref, coh_ref, curv_ref, raw_u, raw_k, send1, recv1, send2, recv2, load_sem, out1, in1, out2, in2):
    batch = lax.axis_index("segment")
    i, n_i = lax.axis_index("inline"), lax.axis_size("inline")
    x, n_x = lax.axis_index("xline"), lax.axis_size("xline")
    has = {LEFT: x > 0, RIGHT: x < n_x - 1, ABOVE: i > 0, BELOW: i < n_i - 1}

    def exists(d):
        parts = [has[part] for part in ((d[0], 0), (0, d[1])) if part != (0, 0)]
        return parts[0] if len(parts) == 1 else parts[0] & parts[1]

    def device(d):
        return {"inline": i + d[0], "xline": x + d[1]}

    load_u = pltpu.make_async_copy(survey_ref.at[batch], raw_u, load_sem.at[0])
    load_k = pltpu.make_async_copy(conduct_ref.at[:, batch], raw_k, load_sem.at[1])
    load_u.start()
    load_k.start()

    barrier = pltpu.get_barrier_semaphore()
    for d in DIRS:

        @pl.when(exists(d))
        def _():
            pl.semaphore_signal(barrier, inc=1, device_id=device(d), device_id_type=MESH)

    def copy(d, table, src, dst, out_sems, in_sems):
        back = (-d[0], -d[1])
        at, n = table[d]
        to, _ = table[back]
        return pltpu.make_async_remote_copy(
            src_ref=src.at[pl.ds(at, n)],
            dst_ref=dst.at[pl.ds(to, n)],
            send_sem=out_sems.at[DIRS.index(d)],
            recv_sem=in_sems.at[DIRS.index(back)],
            device_id=device(d),
            device_id_type=MESH,
        )

    def arrival(d, table, src, dst, out_sems, in_sems):
        at, n = table[d]
        return pltpu.make_async_remote_copy(
            src_ref=src.at[pl.ds(at, n)],
            dst_ref=dst.at[pl.ds(at, n)],
            send_sem=out_sems.at[DIRS.index(d)],
            recv_sem=in_sems.at[DIRS.index(d)],
            device_id=device(d),
            device_id_type=MESH,
        )

    pos = positions()
    width = widths_ref[batch, 0]
    is2, is3, is4 = width == 2, width == 3, width == 4

    def last(v):
        return jnp.where(is2, v[1:2], jnp.where(is3, v[2:3], v[3:4]))

    def at_last(v):
        zero = jnp.zeros_like(v)
        return jnp.concatenate([zero, jnp.where(is2, v, zero), jnp.where(is3, v, zero), jnp.where(is4, v, zero)], 0)

    load_u.wait()
    load_k.wait()
    rows, cols = raw_u.shape[0], raw_u.shape[1]
    shape = (rows, cols, SUB, LANE)
    u = raw_u[...].reshape(shape)
    ki, kx, kt = (raw_k[a].astype(jnp.float32).reshape(shape) for a in range(3))

    ct = kt + later(kt, pos)
    cx = kx[:, 1:] + kx[:, :-1]
    ci = ki[1:] + ki[:-1]
    ci = jnp.concatenate([ci[0:1], jnp.where(width > 2, ci[1:2], 0.0), jnp.where(width > 3, ci[2:3], 0.0)], 0)

    def inner(v):
        ft = ct * (later(v, pos) - v)
        fx = cx * (v[:, 1:] - v[:, :-1])
        fi = ci * (v[1:] - v[:-1])
        total = ft - around(ft, pos)
        total = total + pad_cols(fx, 0, 1) - pad_cols(fx, 1, 0)
        return total + pad_rows(fi, 0, 1) - pad_rows(fi, 1, 0)

    p = u + half_step * inner(u)

    def put(ref, at, value):
        ref[pl.ds(at, value.shape[0])] = value

    ki_last, u_last, kx_last, p_last = last(ki)[0], last(u)[0], last(kx)[0], last(p)[0]
    for d, c in ((LEFT, 0), (RIGHT, cols - 1)):
        at = FIRST[d][0]
        put(send1, at, p[:, c])
        put(send1, at + 4, u[:, c])
        put(send1, at + 8, kx[:, c])
        put(send1, at + 12, ki[0, c : c + 1])
        put(send1, at + 13, ki_last[c : c + 1])
    for d, (pr, ur, kir, kxr) in ((ABOVE, (p[0], u[0], ki[0], kx[0])), (BELOW, (p_last, u_last, ki_last, kx_last))):
        at = FIRST[d][0]
        put(send1, at, pr)
        put(send1, at + 4, ur)
        put(send1, at + 8, kir)
        put(send1, at + 12, kxr[0:1])
        put(send1, at + 13, kxr[cols - 1 :])
        for dx, c in ((-1, 0), (1, cols - 1)):
            at = FIRST[(d[0], dx)][0]
            put(send1, at, ur[c : c + 1])
            put(send1, at + 1, kir[c : c + 1])
            put(send1, at + 2, kxr[c : c + 1])

    expected = (1 + has[LEFT].astype(jnp.int32) + has[RIGHT].astype(jnp.int32)) * (
        1 + has[ABOVE].astype(jnp.int32) + has[BELOW].astype(jnp.int32)
    ) - 1
    pl.semaphore_wait(barrier, expected)

    def send_all(*what):
        for d in DIRS:

            @pl.when(exists(d))
            def _():
                copy(d, *what).start()

    def receive_all(*what):
        for d in DIRS:

            @pl.when(exists(d))
            def _():
                arrival(d, *what).wait_recv()

    def drain(*what):
        for d in DIRS:

            @pl.when(exists(d))
            def _():
                copy(d, *what).wait_send()

    one = (FIRST, send1, recv1, out1, in1)
    two = (SECOND, send2, recv2, out2, in2)
    send_all(*one)
    receive_all(*one)

    def got(d, at, n):
        return recv1[pl.ds(FIRST[d][0] + at, n)]

    def open_to(d, flux):
        return jnp.where(has[d], flux, 0.0)

    side_c, side_u1, side_flux = {}, {}, {}
    for d, c in ((LEFT, 0), (RIGHT, cols - 1)):
        p_d, u_d, kx_d = (got(d, at, rows)[:, None] for at in (0, 4, 8))
        side_c[d] = kx_d + kx[:, c : c + 1]
        flux = open_to(d, side_c[d] * (u_d - u[:, c : c + 1]))
        side_flux[d] = flux
        change = -flux
        corner = (-1, d[1])
        end = open_to(ABOVE, (got(corner, 1, 1) + got(d, 12, 1)) * (got(corner, 0, 1) - u_d[0]))
        change = change + pad_rows(end[None], 0, rows - 1)
        corner = (1, d[1])
        end = open_to(BELOW, (got(corner, 1, 1) + got(d, 13, 1)) * (got(corner, 0, 1) - last(u_d)[0]))
        change = change + at_last(end[None])
        side_u1[d] = p_d + half_step * change
    for d, (ki_r, u_r) in ((ABOVE, (ki[0:1], u[0:1])), (BELOW, (ki_last[None], u_last[None]))):
        p_d, u_d, ki_d = (got(d, at, cols)[None] for at in (0, 4, 8))
        side_c[d] = ki_d + ki_r
        flux = open_to(d, side_c[d] * (u_d - u_r))
        side_flux[d] = flux
        change = -flux
        corner = (d[0], -1)
        end = open_to(LEFT, (got(corner, 2, 1) + got(d, 12, 1)) * (got(corner, 0, 1) - u_d[0, 0:1]))
        change = change + pad_cols(end[None], 0, cols - 1)
        corner = (d[0], 1)
        end = open_to(RIGHT, (got(corner, 2, 1) + got(d, 13, 1)) * (got(corner, 0, 1) - u_d[0, cols - 1 :]))
        change = change + pad_cols(end[None], cols - 1, 0)
        side_u1[d] = p_d + half_step * change

    def outer(flux):
        return (
            pad_cols(flux[LEFT], 0, cols - 1)
            + pad_cols(flux[RIGHT], cols - 1, 0)
            + pad_rows(flux[ABOVE], 0, rows - 1)
            + at_last(flux[BELOW])
        )

    u1 = p + half_step * outer(side_flux)
    u1_edge = {LEFT: u1[:, 0:1], RIGHT: u1[:, cols - 1 :], ABOVE: u1[0:1], BELOW: last(u1)}
    flux2 = {d: open_to(d, side_c[d] * (side_u1[d] - u1_edge[d])) for d in u1_edge}
    u2 = u1 + half_step * (inner(u1) + outer(flux2))

    top = u2[0:2]
    bottom = jnp.where(is2, u2[0:2], jnp.where(is3, u2[1:3], u2[2:4]))

    def flat(v):
        return v.reshape((v.shape[0] * v.shape[1], SUB, LANE))

    put(send2, SECOND[LEFT][0], flat(u2[:, 0:2]))
    put(send2, SECOND[RIGHT][0], flat(u2[:, cols - 2 :]))
    put(send2, SECOND[ABOVE][0], flat(top))
    put(send2, SECOND[BELOW][0], flat(bottom))
    for dx, near, far in ((-1, 0, 1), (1, cols - 1, cols - 2)):
        for di, block, r_near, r_far in ((-1, top, 0, 1), (1, bottom, 1, 0)):
            at = SECOND[(di, dx)][0]
            put(send2, at, block[r_near, near : near + 1])
            put(send2, at + 1, block[r_near, far : far + 1])
            put(send2, at + 2, block[r_far, near : near + 1])
    send_all(*two)
    receive_all(*two)

    def block2(d, r, c):
        return recv2[pl.ds(SECOND[d][0], r * c)].reshape((r, c, SUB, LANE))

    def corner2(d):
        at = SECOND[d][0]
        near, side, row = (recv2[pl.ds(at + j, 1)][None] for j in range(3))
        near_row = [side, near] if d[1] < 0 else [near, side]
        far_row = [row, row]
        near_row, far_row = jnp.concatenate(near_row, 1), jnp.concatenate(far_row, 1)
        return jnp.concatenate([far_row, near_row] if d[0] < 0 else [near_row, far_row], 0)

    own = jnp.concatenate([block2(LEFT, rows, 2), u2, block2(RIGHT, rows, 2)], 1)
    above = jnp.concatenate([corner2((-1, -1)), block2(ABOVE, 2, cols), corner2((-1, 1))], 1)
    below = jnp.concatenate([corner2((1, -1)), block2(BELOW, 2, cols), corner2((1, 1))], 1)
    b0, b1 = below[0:1], below[1:2]
    e = [
        above[0:1],
        jnp.where(has[ABOVE], above[1:2], own[0:1]),
        own[0:1],
        own[1:2],
        jnp.where(is2, b0, own[2:3]),
        jnp.where(is2, b1, jnp.where(is3, b0, own[3:4])),
        jnp.where(is3, b1, b0),
        b1,
    ]
    no_next = jnp.logical_not(has[BELOW])
    closes = {4: no_next & is2, 5: no_next & is3, 6: no_next & is4}

    def close_rows(r):
        return [jnp.where(closes[j], r[j - 1], r[j]) if j in closes else r[j] for j in range(len(r))]

    e = jnp.concatenate(close_rows(e), 0)
    e = jnp.concatenate(
        [
            e[:, 0:1],
            jnp.where(has[LEFT], e[:, 1:2], e[:, 2:3]),
            e[:, 2:6],
            jnp.where(has[RIGHT], e[:, 6:7], e[:, 5:6]),
            e[:, 7:8],
        ],
        1,
    )
    mid = e[1:7, 1:7]
    gi = e[2:8, 1:7] - e[0:6, 1:7]
    gx = e[1:7, 2:8] - e[1:7, 0:6]
    gt = later(mid, pos) - earlier(mid, pos)

    def close(g):
        r = [None] + [g[j : j + 1] for j in range(6)]
        r[1] = jnp.where(has[ABOVE], r[1], r[2])
        g = jnp.concatenate(close_rows(r)[1:], 0)
        return jnp.concatenate(
            [jnp.where(has[LEFT], g[:, 0:1], g[:, 1:2]), g[:, 1:5], jnp.where(has[RIGHT], g[:, 5:6], g[:, 4:5])], 1
        )

    gi, gx, gt = close(gi), close(gx), close(gt)

    def smoothed(v):
        v = v[0:5] + v[1:6]
        v = v[0:4] + v[1:5]
        v = v[:, 0:5] + v[:, 1:6]
        v = v[:, 0:4] + v[:, 1:5]
        return (1.0 / 256.0) * (later(v, pos) + 2.0 * v + earlier(v, pos))

    j11, j22, j33 = smoothed(gi * gi), smoothed(gx * gx), smoothed(gt * gt)
    j12, j13, j23 = smoothed(gi * gx), smoothed(gi * gt), smoothed(gx * gt)
    trace = j11 + j22 + j33
    minors = j11 * j22 - j12 * j12 + j11 * j33 - j13 * j13 + j22 * j33 - j23 * j23
    coherence = 1.0 - 3.0 * minors / (trace * trace + epsilon)
    gi, gx = gi[1:5, 1:5], gx[1:5, 1:5]
    inside = e[2:6, 2:6]
    second = e[3:7, 2:6] + e[1:5, 2:6] + e[2:6, 3:7] + e[2:6, 1:5] - 4.0 * inside
    root = lax.rsqrt(1.0 + 0.25 * (gi * gi + gx * gx))
    curvature = second * (root * root * root)
    for r in range(rows):
        coh_ref[r] = jnp.where(r < width, coherence[r], 0.0)
        curv_ref[r] = jnp.where(r < width, curvature[r], 0.0)
    drain(*one)
    drain(*two)


def on_device(survey, conduct, widths):
    _, rows, cols, samples = survey.shape
    traces = jax.ShapeDtypeStruct((rows, cols, SUB, LANE), jnp.float32)
    vmem = pl.BlockSpec(memory_space=pltpu.VMEM)
    hbm = pl.BlockSpec(memory_space=pl.ANY)
    buffer = lambda n: pltpu.VMEM((n, SUB, LANE), jnp.float32)
    coherence, curvature = pl.pallas_call(
        kernel,
        out_shape=(traces, traces),
        in_specs=[pl.BlockSpec(memory_space=pltpu.SMEM), hbm, hbm],
        out_specs=(vmem, vmem),
        scratch_shapes=[
            pltpu.VMEM((rows, cols, samples), jnp.float32),
            pltpu.VMEM((3, rows, cols, samples), jnp.bfloat16),
            buffer(FIRST_LEN),
            buffer(FIRST_LEN),
            buffer(SECOND_LEN),
            buffer(SECOND_LEN),
            pltpu.SemaphoreType.DMA((2,)),
            pltpu.SemaphoreType.DMA((8,)),
            pltpu.SemaphoreType.DMA((8,)),
            pltpu.SemaphoreType.DMA((8,)),
            pltpu.SemaphoreType.DMA((8,)),
        ],
        compiler_params=pltpu.CompilerParams(
            collective_id=0, has_side_effects=True, vmem_limit_bytes=32 * 1024 * 1024
        ),
    )(widths, survey, conduct)
    shape = (1, rows, cols, samples)
    return coherence.reshape(shape), curvature.reshape(shape)


def solution(mesh):
    placed = (
        P(None, "inline", "xline", None),
        P(None, None, "inline", "xline", None),
        P(None, "inline"),
    )
    return jax.shard_map(
        on_device,
        mesh=mesh,
        in_specs=placed,
        out_specs=(P("segment", "inline", "xline", None), P("segment", "inline", "xline", None)),
        check_vma=False,
    )
```

```python
import jax
import jax.numpy as jnp
from jax import lax
from jax.experimental import pallas as pl
from jax.experimental.pallas import tpu as pltpu
from jax.sharding import PartitionSpec as P

MESH = pl.DeviceIdType.MESH
step_size = 0.15
epsilon = 1e-06
half_step = 0.5 * step_size
SUB, LANE = 8, 128

LEFT, RIGHT, ABOVE, BELOW = (0, -1), (0, 1), (-1, 0), (1, 0)
DIRS = [(-1, -1), (-1, 1), (1, -1), (1, 1), LEFT, RIGHT, ABOVE, BELOW]


def slots(side, corner):
    table, at = {}, 0
    for d in DIRS:
        n = corner if d[0] and d[1] else side
        table[d] = (at, n)
        at += n
    return table, at


FIRST, FIRST_LEN = slots(14, 3)
SECOND, SECOND_LEN = slots(8, 3)


def positions():
    lane = lax.broadcasted_iota(jnp.int32, (SUB, LANE), 1)
    sub = lax.broadcasted_iota(jnp.int32, (SUB, LANE), 0)
    return lane == 0, lane == LANE - 1, (lane == 0) & (sub == 0), (lane == LANE - 1) & (sub == SUB - 1)


def later(v, pos):
    n = v.ndim
    rolled = pltpu.roll(v, LANE - 1, n - 1)
    v_next = jnp.where(pos[1], pltpu.roll(rolled, SUB - 1, n - 2), rolled)
    return jnp.where(pos[3], v, v_next)


def around(v, pos):
    n = v.ndim
    rolled = pltpu.roll(v, 1, n - 1)
    return jnp.where(pos[0], pltpu.roll(rolled, 1, n - 2), rolled)


def earlier(v, pos):
    return jnp.where(pos[2], v, around(v, pos))


def pad_rows(value, before, after):
    zero = jnp.zeros((1,) + value.shape[1:], value.dtype)
    return jnp.concatenate([zero] * before + [value] + [zero] * after, 0)


def pad_cols(value, before, after):
    zero = jnp.zeros((value.shape[0], 1) + value.shape[2:], value.dtype)
    return jnp.concatenate([zero] * before + [value] + [zero] * after, 1)


def kernel(widths_ref, survey_ref, conduct_ref, coh_ref, curv_ref, raw_u, raw_k, send1, recv1, send2, recv2, load_sem, out1, in1, out2, in2):
    batch = lax.axis_index("segment")
    i, n_i = lax.axis_index("inline"), lax.axis_size("inline")
    x, n_x = lax.axis_index("xline"), lax.axis_size("xline")
    has = {LEFT: x > 0, RIGHT: x < n_x - 1, ABOVE: i > 0, BELOW: i < n_i - 1}

    def exists(d):
        parts = [has[part] for part in ((d[0], 0), (0, d[1])) if part != (0, 0)]
        return parts[0] if len(parts) == 1 else parts[0] & parts[1]

    def device(d):
        return {"inline": i + d[0], "xline": x + d[1]}

    load_u = pltpu.make_async_copy(survey_ref.at[batch], raw_u, load_sem.at[0])
    load_k = pltpu.make_async_copy(conduct_ref.at[:, batch], raw_k, load_sem.at[1])
    load_u.start()
    load_k.start()

    barrier = pltpu.get_barrier_semaphore()
    for d in DIRS:

        @pl.when(exists(d))
        def _():
            pl.semaphore_signal(barrier, inc=1, device_id=device(d), device_id_type=MESH)

    def copy(d, table, src, dst, out_sems, in_sems):
        back = (-d[0], -d[1])
        at, n = table[d]
        to, _ = table[back]
        return pltpu.make_async_remote_copy(
            src_ref=src.at[pl.ds(at, n)],
            dst_ref=dst.at[pl.ds(to, n)],
            send_sem=out_sems.at[DIRS.index(d)],
            recv_sem=in_sems.at[DIRS.index(back)],
            device_id=device(d),
            device_id_type=MESH,
        )

    def arrival(d, table, src, dst, out_sems, in_sems):
        at, n = table[d]
        return pltpu.make_async_remote_copy(
            src_ref=src.at[pl.ds(at, n)],
            dst_ref=dst.at[pl.ds(at, n)],
            send_sem=out_sems.at[DIRS.index(d)],
            recv_sem=in_sems.at[DIRS.index(d)],
            device_id=device(d),
            device_id_type=MESH,
        )

    pos = positions()
    width = widths_ref[0, batch]
    is2, is3, is4 = width == 2, width == 3, width == 4

    def last(v):
        return jnp.where(is2, v[1:2], jnp.where(is3, v[2:3], v[3:4]))

    def at_last(v):
        zero = jnp.zeros_like(v)
        return jnp.concatenate([zero, jnp.where(is2, v, zero), jnp.where(is3, v, zero), jnp.where(is4, v, zero)], 0)

    load_u.wait()
    load_k.wait()
    rows, cols = raw_u.shape[0], raw_u.shape[1]
    shape = (rows, cols, SUB, LANE)
    u = raw_u[...].reshape(shape)
    ki, kx, kt = (raw_k[a].astype(jnp.float32).reshape(shape) for a in range(3))

    ct = kt + later(kt, pos)
    cx = kx[:, 1:] + kx[:, :-1]
    ci = ki[1:] + ki[:-1]
    ci = jnp.concatenate([ci[0:1], jnp.where(width > 2, ci[1:2], 0.0), jnp.where(width > 3, ci[2:3], 0.0)], 0)

    def inner(v):
        ft = ct * (later(v, pos) - v)
        fx = cx * (v[:, 1:] - v[:, :-1])
        fi = ci * (v[1:] - v[:-1])
        total = ft - around(ft, pos)
        total = total + pad_cols(fx, 0, 1) - pad_cols(fx, 1, 0)
        return total + pad_rows(fi, 0, 1) - pad_rows(fi, 1, 0)

    p = u + half_step * inner(u)

    def put(ref, at, value):
        ref[pl.ds(at, value.shape[0])] = value

    ki_last, u_last, kx_last, p_last = last(ki)[0], last(u)[0], last(kx)[0], last(p)[0]
    for d, c in ((LEFT, 0), (RIGHT, cols - 1)):
        at = FIRST[d][0]
        put(send1, at, p[:, c])
        put(send1, at + 4, u[:, c])
        put(send1, at + 8, kx[:, c])
        put(send1, at + 12, ki[0, c : c + 1])
        put(send1, at + 13, ki_last[c : c + 1])
    for d, (pr, ur, kir, kxr) in ((ABOVE, (p[0], u[0], ki[0], kx[0])), (BELOW, (p_last, u_last, ki_last, kx_last))):
        at = FIRST[d][0]
        put(send1, at, pr)
        put(send1, at + 4, ur)
        put(send1, at + 8, kir)
        put(send1, at + 12, kxr[0:1])
        put(send1, at + 13, kxr[cols - 1 :])
        for dx, c in ((-1, 0), (1, cols - 1)):
            at = FIRST[(d[0], dx)][0]
            put(send1, at, ur[c : c + 1])
            put(send1, at + 1, kir[c : c + 1])
            put(send1, at + 2, kxr[c : c + 1])

    expected = (1 + has[LEFT].astype(jnp.int32) + has[RIGHT].astype(jnp.int32)) * (
        1 + has[ABOVE].astype(jnp.int32) + has[BELOW].astype(jnp.int32)
    ) - 1
    pl.semaphore_wait(barrier, expected)

    def send_all(*what):
        for d in DIRS:

            @pl.when(exists(d))
            def _():
                copy(d, *what).start()

    def receive_all(*what):
        for d in DIRS:

            @pl.when(exists(d))
            def _():
                arrival(d, *what).wait_recv()

    def drain(*what):
        for d in DIRS:

            @pl.when(exists(d))
            def _():
                copy(d, *what).wait_send()

    one = (FIRST, send1, recv1, out1, in1)
    two = (SECOND, send2, recv2, out2, in2)
    send_all(*one)
    receive_all(*one)

    def got(d, at, n):
        return recv1[pl.ds(FIRST[d][0] + at, n)]

    def open_to(d, flux):
        return jnp.where(has[d], flux, 0.0)

    side_c, side_u1, side_flux = {}, {}, {}
    for d, c in ((LEFT, 0), (RIGHT, cols - 1)):
        p_d, u_d, kx_d = (got(d, at, rows)[:, None] for at in (0, 4, 8))
        side_c[d] = kx_d + kx[:, c : c + 1]
        flux = open_to(d, side_c[d] * (u_d - u[:, c : c + 1]))
        side_flux[d] = flux
        change = -flux
        corner = (-1, d[1])
        end = open_to(ABOVE, (got(corner, 1, 1) + got(d, 12, 1)) * (got(corner, 0, 1) - u_d[0]))
        change = change + pad_rows(end[None], 0, rows - 1)
        corner = (1, d[1])
        end = open_to(BELOW, (got(corner, 1, 1) + got(d, 13, 1)) * (got(corner, 0, 1) - last(u_d)[0]))
        change = change + at_last(end[None])
        side_u1[d] = p_d + half_step * change
    for d, (ki_r, u_r) in ((ABOVE, (ki[0:1], u[0:1])), (BELOW, (ki_last[None], u_last[None]))):
        p_d, u_d, ki_d = (got(d, at, cols)[None] for at in (0, 4, 8))
        side_c[d] = ki_d + ki_r
        flux = open_to(d, side_c[d] * (u_d - u_r))
        side_flux[d] = flux
        change = -flux
        corner = (d[0], -1)
        end = open_to(LEFT, (got(corner, 2, 1) + got(d, 12, 1)) * (got(corner, 0, 1) - u_d[0, 0:1]))
        change = change + pad_cols(end[None], 0, cols - 1)
        corner = (d[0], 1)
        end = open_to(RIGHT, (got(corner, 2, 1) + got(d, 13, 1)) * (got(corner, 0, 1) - u_d[0, cols - 1 :]))
        change = change + pad_cols(end[None], cols - 1, 0)
        side_u1[d] = p_d + half_step * change

    def outer(flux):
        return (
            pad_cols(flux[LEFT], 0, cols - 1)
            + pad_cols(flux[RIGHT], cols - 1, 0)
            + pad_rows(flux[ABOVE], 0, rows - 1)
            + at_last(flux[BELOW])
        )

    u1 = p + half_step * outer(side_flux)
    u1_edge = {LEFT: u1[:, 0:1], RIGHT: u1[:, cols - 1 :], ABOVE: u1[0:1], BELOW: last(u1)}
    flux2 = {d: open_to(d, side_c[d] * (side_u1[d] - u1_edge[d])) for d in u1_edge}
    u2 = u1 + half_step * (inner(u1) + outer(flux2))

    top = u2[0:2]
    bottom = jnp.where(is2, u2[0:2], jnp.where(is3, u2[1:3], u2[2:4]))

    def flat(v):
        return v.reshape((v.shape[0] * v.shape[1], SUB, LANE))

    put(send2, SECOND[LEFT][0], flat(u2[:, 0:2]))
    put(send2, SECOND[RIGHT][0], flat(u2[:, cols - 2 :]))
    put(send2, SECOND[ABOVE][0], flat(top))
    put(send2, SECOND[BELOW][0], flat(bottom))
    for dx, near, far in ((-1, 0, 1), (1, cols - 1, cols - 2)):
        for di, block, r_near, r_far in ((-1, top, 0, 1), (1, bottom, 1, 0)):
            at = SECOND[(di, dx)][0]
            put(send2, at, block[r_near, near : near + 1])
            put(send2, at + 1, block[r_near, far : far + 1])
            put(send2, at + 2, block[r_far, near : near + 1])
    send_all(*two)
    receive_all(*two)

    def block2(d, r, c):
        return recv2[pl.ds(SECOND[d][0], r * c)].reshape((r, c, SUB, LANE))

    def corner2(d):
        at = SECOND[d][0]
        near, side, row = (recv2[pl.ds(at + j, 1)][None] for j in range(3))
        near_row = [side, near] if d[1] < 0 else [near, side]
        far_row = [row, row]
        near_row, far_row = jnp.concatenate(near_row, 1), jnp.concatenate(far_row, 1)
        return jnp.concatenate([far_row, near_row] if d[0] < 0 else [near_row, far_row], 0)

    own = jnp.concatenate([block2(LEFT, rows, 2), u2, block2(RIGHT, rows, 2)], 1)
    above = jnp.concatenate([corner2((-1, -1)), block2(ABOVE, 2, cols), corner2((-1, 1))], 1)
    below = jnp.concatenate([corner2((1, -1)), block2(BELOW, 2, cols), corner2((1, 1))], 1)
    b0, b1 = below[0:1], below[1:2]
    e = [
        above[0:1],
        jnp.where(has[ABOVE], above[1:2], own[0:1]),
        own[0:1],
        own[1:2],
        jnp.where(is2, b0, own[2:3]),
        jnp.where(is2, b1, jnp.where(is3, b0, own[3:4])),
        jnp.where(is3, b1, b0),
        b1,
    ]
    no_next = jnp.logical_not(has[BELOW])
    closes = {4: no_next & is2, 5: no_next & is3, 6: no_next & is4}

    def close_rows(r):
        return [jnp.where(closes[j], r[j - 1], r[j]) if j in closes else r[j] for j in range(len(r))]

    e = jnp.concatenate(close_rows(e), 0)
    e = jnp.concatenate(
        [
            e[:, 0:1],
            jnp.where(has[LEFT], e[:, 1:2], e[:, 2:3]),
            e[:, 2:6],
            jnp.where(has[RIGHT], e[:, 6:7], e[:, 5:6]),
            e[:, 7:8],
        ],
        1,
    )
    mid = e[1:7, 1:7]
    gi = e[2:8, 1:7] - e[0:6, 1:7]
    gx = e[1:7, 2:8] - e[1:7, 0:6]
    gt = later(mid, pos) - earlier(mid, pos)

    def close(g):
        r = [None] + [g[j : j + 1] for j in range(6)]
        r[1] = jnp.where(has[ABOVE], r[1], r[2])
        g = jnp.concatenate(close_rows(r)[1:], 0)
        return jnp.concatenate(
            [jnp.where(has[LEFT], g[:, 0:1], g[:, 1:2]), g[:, 1:5], jnp.where(has[RIGHT], g[:, 5:6], g[:, 4:5])], 1
        )

    gi, gx, gt = close(gi), close(gx), close(gt)

    def smoothed(v):
        v = v[0:5] + v[1:6]
        v = v[0:4] + v[1:5]
        v = v[:, 0:5] + v[:, 1:6]
        v = v[:, 0:4] + v[:, 1:5]
        return (1.0 / 256.0) * (later(v, pos) + 2.0 * v + earlier(v, pos))

    j11, j22, j33 = smoothed(gi * gi), smoothed(gx * gx), smoothed(gt * gt)
    j12, j13, j23 = smoothed(gi * gx), smoothed(gi * gt), smoothed(gx * gt)
    trace = j11 + j22 + j33
    minors = j11 * j22 - j12 * j12 + j11 * j33 - j13 * j13 + j22 * j33 - j23 * j23
    coherence = 1.0 - 3.0 * minors / (trace * trace + epsilon)
    gi, gx = gi[1:5, 1:5], gx[1:5, 1:5]
    inside = e[2:6, 2:6]
    second = e[3:7, 2:6] + e[1:5, 2:6] + e[2:6, 3:7] + e[2:6, 1:5] - 4.0 * inside
    root = lax.rsqrt(1.0 + 0.25 * (gi * gi + gx * gx))
    curvature = second * (root * root * root)
    for r in range(rows):
        coh_ref[r] = jnp.where(r < width, coherence[r], 0.0)
        curv_ref[r] = jnp.where(r < width, curvature[r], 0.0)
    drain(*one)
    drain(*two)


def on_device(survey, conduct, widths):
    _, rows, cols, samples = survey.shape
    traces = jax.ShapeDtypeStruct((rows, cols, SUB, LANE), jnp.float32)
    vmem = pl.BlockSpec(memory_space=pltpu.VMEM)
    hbm = pl.BlockSpec(memory_space=pl.ANY)
    buffer = lambda n: pltpu.VMEM((n, SUB, LANE), jnp.float32)
    coherence, curvature = pl.pallas_call(
        kernel,
        out_shape=(traces, traces),
        in_specs=[pl.BlockSpec(memory_space=pltpu.SMEM), hbm, hbm],
        out_specs=(vmem, vmem),
        scratch_shapes=[
            pltpu.VMEM((rows, cols, samples), jnp.float32),
            pltpu.VMEM((3, rows, cols, samples), jnp.bfloat16),
            buffer(FIRST_LEN),
            buffer(FIRST_LEN),
            buffer(SECOND_LEN),
            buffer(SECOND_LEN),
            pltpu.SemaphoreType.DMA((2,)),
            pltpu.SemaphoreType.DMA((8,)),
            pltpu.SemaphoreType.DMA((8,)),
            pltpu.SemaphoreType.DMA((8,)),
            pltpu.SemaphoreType.DMA((8,)),
        ],
        compiler_params=pltpu.CompilerParams(
            collective_id=0, has_side_effects=True, vmem_limit_bytes=55000 * 1024
        ),
    )(widths.T, survey, conduct)
    shape = (1, rows, cols, samples)
    return coherence.reshape(shape), curvature.reshape(shape)


def solution(mesh):
    placed = (
        P(None, "inline", "xline", None),
        P(None, None, "inline", "xline", None),
        P(None, "inline"),
    )
    return jax.shard_map(
        on_device,
        mesh=mesh,
        in_specs=placed,
        out_specs=(P("segment", "inline", "xline", None), P("segment", "inline", "xline", None)),
        check_vma=False,
    )
```

```python
import jax
import jax.numpy as jnp
from jax import lax
from jax.experimental import pallas as pl
from jax.experimental.pallas import tpu as pltpu
from jax.sharding import PartitionSpec as P

MESH = pl.DeviceIdType.MESH
step_size = 0.15
epsilon = 1e-06
half_step = 0.5 * step_size
SUB, LANE = 8, 128

LEFT, RIGHT, ABOVE, BELOW = (0, -1), (0, 1), (-1, 0), (1, 0)
DIRS = [(-1, -1), (-1, 1), (1, -1), (1, 1), LEFT, RIGHT, ABOVE, BELOW]


def slots(side, corner):
    table, at = {}, 0
    for d in DIRS:
        n = corner if d[0] and d[1] else side
        table[d] = (at, n)
        at += n
    return table, at


FIRST, FIRST_LEN = slots(14, 3)
SECOND, SECOND_LEN = slots(8, 3)


def positions():
    lane = lax.broadcasted_iota(jnp.int32, (SUB, LANE), 1)
    sub = lax.broadcasted_iota(jnp.int32, (SUB, LANE), 0)
    return lane == 0, lane == LANE - 1, (lane == 0) & (sub == 0), (lane == LANE - 1) & (sub == SUB - 1)


def later(v, pos):
    n = v.ndim
    rolled = pltpu.roll(v, LANE - 1, n - 1)
    v_next = jnp.where(pos[1], pltpu.roll(rolled, SUB - 1, n - 2), rolled)
    return jnp.where(pos[3], v, v_next)


def around(v, pos):
    n = v.ndim
    rolled = pltpu.roll(v, 1, n - 1)
    return jnp.where(pos[0], pltpu.roll(rolled, 1, n - 2), rolled)


def earlier(v, pos):
    return jnp.where(pos[2], v, around(v, pos))


def pad_rows(value, before, after):
    zero = jnp.zeros((1,) + value.shape[1:], value.dtype)
    return jnp.concatenate([zero] * before + [value] + [zero] * after, 0)


def pad_cols(value, before, after):
    zero = jnp.zeros((value.shape[0], 1) + value.shape[2:], value.dtype)
    return jnp.concatenate([zero] * before + [value] + [zero] * after, 1)


def kernel(widths_ref, survey_ref, conduct_ref, coh_ref, raw_u, raw_k, send1, recv1, send2, recv2, load_sem, out1, in1, out2, in2):
    batch = lax.axis_index("segment")
    i, n_i = lax.axis_index("inline"), lax.axis_size("inline")
    x, n_x = lax.axis_index("xline"), lax.axis_size("xline")
    has = {LEFT: x > 0, RIGHT: x < n_x - 1, ABOVE: i > 0, BELOW: i < n_i - 1}

    def exists(d):
        parts = [has[part] for part in ((d[0], 0), (0, d[1])) if part != (0, 0)]
        return parts[0] if len(parts) == 1 else parts[0] & parts[1]

    def device(d):
        return {"inline": i + d[0], "xline": x + d[1]}

    load_u = pltpu.make_async_copy(survey_ref.at[batch], raw_u, load_sem.at[0])
    load_k = pltpu.make_async_copy(conduct_ref.at[:, batch], raw_k, load_sem.at[1])
    load_u.start()
    load_k.start()

    barrier = pltpu.get_barrier_semaphore()
    for d in DIRS:

        @pl.when(exists(d))
        def _():
            pl.semaphore_signal(barrier, inc=1, device_id=device(d), device_id_type=MESH)

    def copy(d, table, src, dst, out_sems, in_sems):
        back = (-d[0], -d[1])
        at, n = table[d]
        to, _ = table[back]
        return pltpu.make_async_remote_copy(
            src_ref=src.at[pl.ds(at, n)],
            dst_ref=dst.at[pl.ds(to, n)],
            send_sem=out_sems.at[DIRS.index(d)],
            recv_sem=in_sems.at[DIRS.index(back)],
            device_id=device(d),
            device_id_type=MESH,
        )

    def arrival(d, table, src, dst, out_sems, in_sems):
        at, n = table[d]
        return pltpu.make_async_remote_copy(
            src_ref=src.at[pl.ds(at, n)],
            dst_ref=dst.at[pl.ds(at, n)],
            send_sem=out_sems.at[DIRS.index(d)],
            recv_sem=in_sems.at[DIRS.index(d)],
            device_id=device(d),
            device_id_type=MESH,
        )

    pos = positions()
    width = widths_ref[0, batch]
    is2, is3, is4 = width == 2, width == 3, width == 4

    def last(v):
        return jnp.where(is2, v[1:2], jnp.where(is3, v[2:3], v[3:4]))

    def at_last(v):
        zero = jnp.zeros_like(v)
        return jnp.concatenate([zero, jnp.where(is2, v, zero), jnp.where(is3, v, zero), jnp.where(is4, v, zero)], 0)

    load_u.wait()
    load_k.wait()
    rows, cols = raw_u.shape[0], raw_u.shape[1]
    shape = (rows, cols, SUB, LANE)
    u = raw_u[...].reshape(shape)
    ki, kx, kt = (raw_k[a].astype(jnp.float32).reshape(shape) for a in range(3))

    ct = kt + later(kt, pos)
    cx = kx[:, 1:] + kx[:, :-1]
    ci = ki[1:] + ki[:-1]
    ci = jnp.concatenate([ci[0:1], jnp.where(width > 2, ci[1:2], 0.0), jnp.where(width > 3, ci[2:3], 0.0)], 0)

    def inner(v):
        ft = ct * (later(v, pos) - v)
        fx = cx * (v[:, 1:] - v[:, :-1])
        fi = ci * (v[1:] - v[:-1])
        total = ft - around(ft, pos)
        total = total + pad_cols(fx, 0, 1) - pad_cols(fx, 1, 0)
        return total + pad_rows(fi, 0, 1) - pad_rows(fi, 1, 0)

    p = u + half_step * inner(u)

    def put(ref, at, value):
        ref[pl.ds(at, value.shape[0])] = value

    ki_last, u_last, kx_last, p_last = last(ki)[0], last(u)[0], last(kx)[0], last(p)[0]
    for d, c in ((LEFT, 0), (RIGHT, cols - 1)):
        at = FIRST[d][0]
        put(send1, at, p[:, c])
        put(send1, at + 4, u[:, c])
        put(send1, at + 8, kx[:, c])
        put(send1, at + 12, ki[0, c : c + 1])
        put(send1, at + 13, ki_last[c : c + 1])
    for d, (pr, ur, kir, kxr) in ((ABOVE, (p[0], u[0], ki[0], kx[0])), (BELOW, (p_last, u_last, ki_last, kx_last))):
        at = FIRST[d][0]
        put(send1, at, pr)
        put(send1, at + 4, ur)
        put(send1, at + 8, kir)
        put(send1, at + 12, kxr[0:1])
        put(send1, at + 13, kxr[cols - 1 :])
        for dx, c in ((-1, 0), (1, cols - 1)):
            at = FIRST[(d[0], dx)][0]
            put(send1, at, ur[c : c + 1])
            put(send1, at + 1, kir[c : c + 1])
            put(send1, at + 2, kxr[c : c + 1])

    expected = (1 + has[LEFT].astype(jnp.int32) + has[RIGHT].astype(jnp.int32)) * (
        1 + has[ABOVE].astype(jnp.int32) + has[BELOW].astype(jnp.int32)
    ) - 1
    pl.semaphore_wait(barrier, expected)

    def send_all(*what):
        for d in DIRS:

            @pl.when(exists(d))
            def _():
                copy(d, *what).start()

    def receive_all(*what):
        for d in DIRS:

            @pl.when(exists(d))
            def _():
                arrival(d, *what).wait_recv()

    def drain(*what):
        for d in DIRS:

            @pl.when(exists(d))
            def _():
                copy(d, *what).wait_send()

    one = (FIRST, send1, recv1, out1, in1)
    two = (SECOND, send2, recv2, out2, in2)
    send_all(*one)
    receive_all(*one)

    def got(d, at, n):
        return recv1[pl.ds(FIRST[d][0] + at, n)]

    def open_to(d, flux):
        return jnp.where(has[d], flux, 0.0)

    side_c, side_u1, side_flux = {}, {}, {}
    for d, c in ((LEFT, 0), (RIGHT, cols - 1)):
        p_d, u_d, kx_d = (got(d, at, rows)[:, None] for at in (0, 4, 8))
        side_c[d] = kx_d + kx[:, c : c + 1]
        flux = open_to(d, side_c[d] * (u_d - u[:, c : c + 1]))
        side_flux[d] = flux
        change = -flux
        corner = (-1, d[1])
        end = open_to(ABOVE, (got(corner, 1, 1) + got(d, 12, 1)) * (got(corner, 0, 1) - u_d[0]))
        change = change + pad_rows(end[None], 0, rows - 1)
        corner = (1, d[1])
        end = open_to(BELOW, (got(corner, 1, 1) + got(d, 13, 1)) * (got(corner, 0, 1) - last(u_d)[0]))
        change = change + at_last(end[None])
        side_u1[d] = p_d + half_step * change
    for d, (ki_r, u_r) in ((ABOVE, (ki[0:1], u[0:1])), (BELOW, (ki_last[None], u_last[None]))):
        p_d, u_d, ki_d = (got(d, at, cols)[None] for at in (0, 4, 8))
        side_c[d] = ki_d + ki_r
        flux = open_to(d, side_c[d] * (u_d - u_r))
        side_flux[d] = flux
        change = -flux
        corner = (d[0], -1)
        end = open_to(LEFT, (got(corner, 2, 1) + got(d, 12, 1)) * (got(corner, 0, 1) - u_d[0, 0:1]))
        change = change + pad_cols(end[None], 0, cols - 1)
        corner = (d[0], 1)
        end = open_to(RIGHT, (got(corner, 2, 1) + got(d, 13, 1)) * (got(corner, 0, 1) - u_d[0, cols - 1 :]))
        change = change + pad_cols(end[None], cols - 1, 0)
        side_u1[d] = p_d + half_step * change

    def outer(flux):
        return (
            pad_cols(flux[LEFT], 0, cols - 1)
            + pad_cols(flux[RIGHT], cols - 1, 0)
            + pad_rows(flux[ABOVE], 0, rows - 1)
            + at_last(flux[BELOW])
        )

    u1 = p + half_step * outer(side_flux)
    u1_edge = {LEFT: u1[:, 0:1], RIGHT: u1[:, cols - 1 :], ABOVE: u1[0:1], BELOW: last(u1)}
    flux2 = {d: open_to(d, side_c[d] * (side_u1[d] - u1_edge[d])) for d in u1_edge}
    u2 = u1 + half_step * (inner(u1) + outer(flux2))

    top = u2[0:2]
    bottom = jnp.where(is2, u2[0:2], jnp.where(is3, u2[1:3], u2[2:4]))

    def flat(v):
        return v.reshape((v.shape[0] * v.shape[1], SUB, LANE))

    put(send2, SECOND[LEFT][0], flat(u2[:, 0:2]))
    put(send2, SECOND[RIGHT][0], flat(u2[:, cols - 2 :]))
    put(send2, SECOND[ABOVE][0], flat(top))
    put(send2, SECOND[BELOW][0], flat(bottom))
    for dx, near, far in ((-1, 0, 1), (1, cols - 1, cols - 2)):
        for di, block, r_near, r_far in ((-1, top, 0, 1), (1, bottom, 1, 0)):
            at = SECOND[(di, dx)][0]
            put(send2, at, block[r_near, near : near + 1])
            put(send2, at + 1, block[r_near, far : far + 1])
            put(send2, at + 2, block[r_far, near : near + 1])
    send_all(*two)
    receive_all(*two)

    def block2(d, r, c):
        return recv2[pl.ds(SECOND[d][0], r * c)].reshape((r, c, SUB, LANE))

    def corner2(d):
        at = SECOND[d][0]
        near, side, row = (recv2[pl.ds(at + j, 1)][None] for j in range(3))
        near_row = [side, near] if d[1] < 0 else [near, side]
        far_row = [row, row]
        near_row, far_row = jnp.concatenate(near_row, 1), jnp.concatenate(far_row, 1)
        return jnp.concatenate([far_row, near_row] if d[0] < 0 else [near_row, far_row], 0)

    own = jnp.concatenate([block2(LEFT, rows, 2), u2, block2(RIGHT, rows, 2)], 1)
    above = jnp.concatenate([corner2((-1, -1)), block2(ABOVE, 2, cols), corner2((-1, 1))], 1)
    below = jnp.concatenate([corner2((1, -1)), block2(BELOW, 2, cols), corner2((1, 1))], 1)
    b0, b1 = below[0:1], below[1:2]
    e = [
        above[0:1],
        jnp.where(has[ABOVE], above[1:2], own[0:1]),
        own[0:1],
        own[1:2],
        jnp.where(is2, b0, own[2:3]),
        jnp.where(is2, b1, jnp.where(is3, b0, own[3:4])),
        jnp.where(is3, b1, b0),
        b1,
    ]
    no_next = jnp.logical_not(has[BELOW])
    closes = {4: no_next & is2, 5: no_next & is3, 6: no_next & is4}

    def close_rows(r):
        return [jnp.where(closes[j], r[j - 1], r[j]) if j in closes else r[j] for j in range(len(r))]

    e = jnp.concatenate(close_rows(e), 0)
    e = jnp.concatenate(
        [
            e[:, 0:1],
            jnp.where(has[LEFT], e[:, 1:2], e[:, 2:3]),
            e[:, 2:6],
            jnp.where(has[RIGHT], e[:, 6:7], e[:, 5:6]),
            e[:, 7:8],
        ],
        1,
    )
    mid = e[1:7, 1:7]
    gi = e[2:8, 1:7] - e[0:6, 1:7]
    gx = e[1:7, 2:8] - e[1:7, 0:6]
    gt = later(mid, pos) - earlier(mid, pos)

    def close(g):
        r = [None] + [g[j : j + 1] for j in range(6)]
        r[1] = jnp.where(has[ABOVE], r[1], r[2])
        g = jnp.concatenate(close_rows(r)[1:], 0)
        return jnp.concatenate(
            [jnp.where(has[LEFT], g[:, 0:1], g[:, 1:2]), g[:, 1:5], jnp.where(has[RIGHT], g[:, 5:6], g[:, 4:5])], 1
        )

    gi, gx, gt = close(gi), close(gx), close(gt)

    def smoothed(v):
        v = v[0:5] + v[1:6]
        v = v[0:4] + v[1:5]
        v = v[:, 0:5] + v[:, 1:6]
        v = v[:, 0:4] + v[:, 1:5]
        return (1.0 / 256.0) * (later(v, pos) + 2.0 * v + earlier(v, pos))

    j11, j22, j33 = smoothed(gi * gi), smoothed(gx * gx), smoothed(gt * gt)
    j12, j13, j23 = smoothed(gi * gx), smoothed(gi * gt), smoothed(gx * gt)
    trace = j11 + j22 + j33
    minors = j11 * j22 - j12 * j12 + j11 * j33 - j13 * j13 + j22 * j33 - j23 * j23
    coherence = 1.0 - 3.0 * minors / (trace * trace + epsilon)
    gi, gx = gi[1:5, 1:5], gx[1:5, 1:5]
    inside = e[2:6, 2:6]
    second = e[3:7, 2:6] + e[1:5, 2:6] + e[2:6, 3:7] + e[2:6, 1:5] - 4.0 * inside
    root = lax.rsqrt(1.0 + 0.25 * (gi * gi + gx * gx))
    curvature = second * (root * root * root)
    for r in range(rows):
        coh_ref[0, r] = jnp.where(r < width, coherence[r], 0.0).reshape((cols, SUB * LANE))
        coh_ref[1, r] = jnp.where(r < width, curvature[r], 0.0).reshape((cols, SUB * LANE))
    drain(*one)
    drain(*two)


def on_device(survey, conduct, widths):
    _, rows, cols, samples = survey.shape
    traces = jax.ShapeDtypeStruct((2, rows, cols, samples), jnp.float32)
    vmem = pl.BlockSpec(memory_space=pltpu.VMEM)
    hbm = pl.BlockSpec(memory_space=pl.ANY)
    buffer = lambda n: pltpu.VMEM((n, SUB, LANE), jnp.float32)
    both = pl.pallas_call(
        kernel,
        out_shape=traces,
        in_specs=[pl.BlockSpec(memory_space=pltpu.SMEM), hbm, hbm],
        out_specs=vmem,
        scratch_shapes=[
            pltpu.VMEM((rows, cols, samples), jnp.float32),
            pltpu.VMEM((3, rows, cols, samples), jnp.bfloat16),
            buffer(FIRST_LEN),
            buffer(FIRST_LEN),
            buffer(SECOND_LEN),
            buffer(SECOND_LEN),
            pltpu.SemaphoreType.DMA((2,)),
            pltpu.SemaphoreType.DMA((8,)),
            pltpu.SemaphoreType.DMA((8,)),
            pltpu.SemaphoreType.DMA((8,)),
            pltpu.SemaphoreType.DMA((8,)),
        ],
        compiler_params=pltpu.CompilerParams(
            collective_id=0, has_side_effects=True, vmem_limit_bytes=55000 * 1024
        ),
    )(widths.T, survey, conduct)
    return both[0:1], both[1:2]


def solution(mesh):
    placed = (
        P(None, "inline", "xline", None),
        P(None, None, "inline", "xline", None),
        P(None, "inline"),
    )
    return jax.shard_map(
        on_device,
        mesh=mesh,
        in_specs=placed,
        out_specs=(P("segment", "inline", "xline", None), P("segment", "inline", "xline", None)),
        check_vma=False,
    )
```

```python
import jax
import jax.numpy as jnp
from jax import lax
from jax.experimental import pallas as pl
from jax.experimental.pallas import tpu as pltpu
from jax.sharding import PartitionSpec as P

MESH = pl.DeviceIdType.MESH
step_size = 0.15
epsilon = 1e-06
half_step = 0.5 * step_size
SUB, LANE = 8, 128

LEFT, RIGHT, ABOVE, BELOW = (0, -1), (0, 1), (-1, 0), (1, 0)
DIRS = [(-1, -1), (-1, 1), (1, -1), (1, 1), LEFT, RIGHT, ABOVE, BELOW]


def slots(side, corner):
    table, at = {}, 0
    for d in DIRS:
        n = corner if d[0] and d[1] else side
        table[d] = (at, n)
        at += n
    return table, at


FIRST, FIRST_LEN = slots(14, 3)
SECOND, SECOND_LEN = slots(8, 3)


def positions():
    lane = lax.broadcasted_iota(jnp.int32, (SUB, LANE), 1)
    sub = lax.broadcasted_iota(jnp.int32, (SUB, LANE), 0)
    return lane == 0, lane == LANE - 1, (lane == 0) & (sub == 0), (lane == LANE - 1) & (sub == SUB - 1)


def later(v, pos):
    n = v.ndim
    rolled = pltpu.roll(v, LANE - 1, n - 1)
    v_next = jnp.where(pos[1], pltpu.roll(rolled, SUB - 1, n - 2), rolled)
    return jnp.where(pos[3], v, v_next)


def around(v, pos):
    n = v.ndim
    rolled = pltpu.roll(v, 1, n - 1)
    return jnp.where(pos[0], pltpu.roll(rolled, 1, n - 2), rolled)


def earlier(v, pos):
    return jnp.where(pos[2], v, around(v, pos))


def pad_rows(value, before, after):
    zero = jnp.zeros((1,) + value.shape[1:], value.dtype)
    return jnp.concatenate([zero] * before + [value] + [zero] * after, 0)


def pad_cols(value, before, after):
    zero = jnp.zeros((value.shape[0], 1) + value.shape[2:], value.dtype)
    return jnp.concatenate([zero] * before + [value] + [zero] * after, 1)


def kernel(widths_ref, survey_ref, conduct_ref, coh_ref, raw_u, raw_k, send1, recv1, send2, recv2, load_sem, out1, in1, out2, in2):
    batch = lax.axis_index("segment")
    i, n_i = lax.axis_index("inline"), lax.axis_size("inline")
    x, n_x = lax.axis_index("xline"), lax.axis_size("xline")
    has = {LEFT: x > 0, RIGHT: x < n_x - 1, ABOVE: i > 0, BELOW: i < n_i - 1}

    def exists(d):
        parts = [has[part] for part in ((d[0], 0), (0, d[1])) if part != (0, 0)]
        return parts[0] if len(parts) == 1 else parts[0] & parts[1]

    def device(d):
        return {"inline": i + d[0], "xline": x + d[1]}

    load_u = pltpu.make_async_copy(survey_ref.at[batch], raw_u, load_sem.at[0])
    load_k = pltpu.make_async_copy(conduct_ref.at[:, batch], raw_k, load_sem.at[1])
    barrier = pltpu.get_barrier_semaphore()
    for d in DIRS:

        @pl.when(exists(d))
        def _():
            pl.semaphore_signal(barrier, inc=1, device_id=device(d), device_id_type=MESH)

    load_u.start()
    load_k.start()

    def copy(d, table, src, dst, out_sems, in_sems):
        back = (-d[0], -d[1])
        at, n = table[d]
        to, _ = table[back]
        return pltpu.make_async_remote_copy(
            src_ref=src.at[pl.ds(at, n)],
            dst_ref=dst.at[pl.ds(to, n)],
            send_sem=out_sems.at[DIRS.index(d)],
            recv_sem=in_sems.at[DIRS.index(back)],
            device_id=device(d),
            device_id_type=MESH,
        )

    def arrival(d, table, src, dst, out_sems, in_sems):
        at, n = table[d]
        return pltpu.make_async_remote_copy(
            src_ref=src.at[pl.ds(at, n)],
            dst_ref=dst.at[pl.ds(at, n)],
            send_sem=out_sems.at[DIRS.index(d)],
            recv_sem=in_sems.at[DIRS.index(d)],
            device_id=device(d),
            device_id_type=MESH,
        )

    pos = positions()
    width = widths_ref[0, batch]
    is2, is3, is4 = width == 2, width == 3, width == 4

    def last(v):
        return jnp.where(is2, v[1:2], jnp.where(is3, v[2:3], v[3:4]))

    def at_last(v):
        zero = jnp.zeros_like(v)
        return jnp.concatenate([zero, jnp.where(is2, v, zero), jnp.where(is3, v, zero), jnp.where(is4, v, zero)], 0)

    load_u.wait()
    load_k.wait()
    rows, cols = raw_u.shape[0], raw_u.shape[1]
    shape = (rows, cols, SUB, LANE)
    u = raw_u[...].reshape(shape)
    ki, kx, kt = (raw_k[a].astype(jnp.float32).reshape(shape) for a in range(3))

    ct = kt + later(kt, pos)
    cx = kx[:, 1:] + kx[:, :-1]
    ci = ki[1:] + ki[:-1]
    ci = jnp.concatenate([ci[0:1], jnp.where(width > 2, ci[1:2], 0.0), jnp.where(width > 3, ci[2:3], 0.0)], 0)

    def inner(v):
        ft = ct * (later(v, pos) - v)
        fx = cx * (v[:, 1:] - v[:, :-1])
        fi = ci * (v[1:] - v[:-1])
        total = ft - around(ft, pos)
        total = total + pad_cols(fx, 0, 1) - pad_cols(fx, 1, 0)
        return total + pad_rows(fi, 0, 1) - pad_rows(fi, 1, 0)

    p = u + half_step * inner(u)

    def put(ref, at, value):
        ref[pl.ds(at, value.shape[0])] = value

    ki_last, u_last, kx_last, p_last = last(ki)[0], last(u)[0], last(kx)[0], last(p)[0]
    for d, c in ((LEFT, 0), (RIGHT, cols - 1)):
        at = FIRST[d][0]
        put(send1, at, p[:, c])
        put(send1, at + 4, u[:, c])
        put(send1, at + 8, kx[:, c])
        put(send1, at + 12, ki[0, c : c + 1])
        put(send1, at + 13, ki_last[c : c + 1])
    for d, (pr, ur, kir, kxr) in ((ABOVE, (p[0], u[0], ki[0], kx[0])), (BELOW, (p_last, u_last, ki_last, kx_last))):
        at = FIRST[d][0]
        put(send1, at, pr)
        put(send1, at + 4, ur)
        put(send1, at + 8, kir)
        put(send1, at + 12, kxr[0:1])
        put(send1, at + 13, kxr[cols - 1 :])
        for dx, c in ((-1, 0), (1, cols - 1)):
            at = FIRST[(d[0], dx)][0]
            put(send1, at, ur[c : c + 1])
            put(send1, at + 1, kir[c : c + 1])
            put(send1, at + 2, kxr[c : c + 1])

    expected = (1 + has[LEFT].astype(jnp.int32) + has[RIGHT].astype(jnp.int32)) * (
        1 + has[ABOVE].astype(jnp.int32) + has[BELOW].astype(jnp.int32)
    ) - 1
    pl.semaphore_wait(barrier, expected)

    def send_all(*what):
        for d in DIRS:

            @pl.when(exists(d))
            def _():
                copy(d, *what).start()

    def receive_all(*what):
        for d in DIRS:

            @pl.when(exists(d))
            def _():
                arrival(d, *what).wait_recv()

    def drain(*what):
        for d in DIRS:

            @pl.when(exists(d))
            def _():
                copy(d, *what).wait_send()

    one = (FIRST, send1, recv1, out1, in1)
    two = (SECOND, send2, recv2, out2, in2)
    send_all(*one)
    receive_all(*one)

    def got(d, at, n):
        return recv1[pl.ds(FIRST[d][0] + at, n)]

    def open_to(d, flux):
        return jnp.where(has[d], flux, 0.0)

    side_c, side_u1, side_flux = {}, {}, {}
    for d, c in ((LEFT, 0), (RIGHT, cols - 1)):
        p_d, u_d, kx_d = (got(d, at, rows)[:, None] for at in (0, 4, 8))
        side_c[d] = kx_d + kx[:, c : c + 1]
        flux = open_to(d, side_c[d] * (u_d - u[:, c : c + 1]))
        side_flux[d] = flux
        change = -flux
        corner = (-1, d[1])
        end = open_to(ABOVE, (got(corner, 1, 1) + got(d, 12, 1)) * (got(corner, 0, 1) - u_d[0]))
        change = change + pad_rows(end[None], 0, rows - 1)
        corner = (1, d[1])
        end = open_to(BELOW, (got(corner, 1, 1) + got(d, 13, 1)) * (got(corner, 0, 1) - last(u_d)[0]))
        change = change + at_last(end[None])
        side_u1[d] = p_d + half_step * change
    for d, (ki_r, u_r) in ((ABOVE, (ki[0:1], u[0:1])), (BELOW, (ki_last[None], u_last[None]))):
        p_d, u_d, ki_d = (got(d, at, cols)[None] for at in (0, 4, 8))
        side_c[d] = ki_d + ki_r
        flux = open_to(d, side_c[d] * (u_d - u_r))
        side_flux[d] = flux
        change = -flux
        corner = (d[0], -1)
        end = open_to(LEFT, (got(corner, 2, 1) + got(d, 12, 1)) * (got(corner, 0, 1) - u_d[0, 0:1]))
        change = change + pad_cols(end[None], 0, cols - 1)
        corner = (d[0], 1)
        end = open_to(RIGHT, (got(corner, 2, 1) + got(d, 13, 1)) * (got(corner, 0, 1) - u_d[0, cols - 1 :]))
        change = change + pad_cols(end[None], cols - 1, 0)
        side_u1[d] = p_d + half_step * change

    def outer(flux):
        return (
            pad_cols(flux[LEFT], 0, cols - 1)
            + pad_cols(flux[RIGHT], cols - 1, 0)
            + pad_rows(flux[ABOVE], 0, rows - 1)
            + at_last(flux[BELOW])
        )

    u1 = p + half_step * outer(side_flux)
    u1_edge = {LEFT: u1[:, 0:1], RIGHT: u1[:, cols - 1 :], ABOVE: u1[0:1], BELOW: last(u1)}
    flux2 = {d: open_to(d, side_c[d] * (side_u1[d] - u1_edge[d])) for d in u1_edge}
    u2 = u1 + half_step * (inner(u1) + outer(flux2))

    top = u2[0:2]
    bottom = jnp.where(is2, u2[0:2], jnp.where(is3, u2[1:3], u2[2:4]))

    def flat(v):
        return v.reshape((v.shape[0] * v.shape[1], SUB, LANE))

    put(send2, SECOND[LEFT][0], flat(u2[:, 0:2]))
    put(send2, SECOND[RIGHT][0], flat(u2[:, cols - 2 :]))
    put(send2, SECOND[ABOVE][0], flat(top))
    put(send2, SECOND[BELOW][0], flat(bottom))
    for dx, near, far in ((-1, 0, 1), (1, cols - 1, cols - 2)):
        for di, block, r_near, r_far in ((-1, top, 0, 1), (1, bottom, 1, 0)):
            at = SECOND[(di, dx)][0]
            put(send2, at, block[r_near, near : near + 1])
            put(send2, at + 1, block[r_near, far : far + 1])
            put(send2, at + 2, block[r_far, near : near + 1])
    send_all(*two)
    receive_all(*two)

    def block2(d, r, c):
        return recv2[pl.ds(SECOND[d][0], r * c)].reshape((r, c, SUB, LANE))

    def corner2(d):
        at = SECOND[d][0]
        near, side, row = (recv2[pl.ds(at + j, 1)][None] for j in range(3))
        near_row = [side, near] if d[1] < 0 else [near, side]
        far_row = [row, row]
        near_row, far_row = jnp.concatenate(near_row, 1), jnp.concatenate(far_row, 1)
        return jnp.concatenate([far_row, near_row] if d[0] < 0 else [near_row, far_row], 0)

    own = jnp.concatenate([block2(LEFT, rows, 2), u2, block2(RIGHT, rows, 2)], 1)
    above = jnp.concatenate([corner2((-1, -1)), block2(ABOVE, 2, cols), corner2((-1, 1))], 1)
    below = jnp.concatenate([corner2((1, -1)), block2(BELOW, 2, cols), corner2((1, 1))], 1)
    b0, b1 = below[0:1], below[1:2]
    e = [
        above[0:1],
        jnp.where(has[ABOVE], above[1:2], own[0:1]),
        own[0:1],
        own[1:2],
        jnp.where(is2, b0, own[2:3]),
        jnp.where(is2, b1, jnp.where(is3, b0, own[3:4])),
        jnp.where(is3, b1, b0),
        b1,
    ]
    no_next = jnp.logical_not(has[BELOW])
    closes = {4: no_next & is2, 5: no_next & is3, 6: no_next & is4}

    def close_rows(r):
        return [jnp.where(closes[j], r[j - 1], r[j]) if j in closes else r[j] for j in range(len(r))]

    e = jnp.concatenate(close_rows(e), 0)
    e = jnp.concatenate(
        [
            e[:, 0:1],
            jnp.where(has[LEFT], e[:, 1:2], e[:, 2:3]),
            e[:, 2:6],
            jnp.where(has[RIGHT], e[:, 6:7], e[:, 5:6]),
            e[:, 7:8],
        ],
        1,
    )
    mid = e[1:7, 1:7]
    gi = e[2:8, 1:7] - e[0:6, 1:7]
    gx = e[1:7, 2:8] - e[1:7, 0:6]
    gt = later(mid, pos) - earlier(mid, pos)

    def close(g):
        r = [None] + [g[j : j + 1] for j in range(6)]
        r[1] = jnp.where(has[ABOVE], r[1], r[2])
        g = jnp.concatenate(close_rows(r)[1:], 0)
        return jnp.concatenate(
            [jnp.where(has[LEFT], g[:, 0:1], g[:, 1:2]), g[:, 1:5], jnp.where(has[RIGHT], g[:, 5:6], g[:, 4:5])], 1
        )

    gi, gx, gt = close(gi), close(gx), close(gt)

    def smoothed(v):
        v = v[0:5] + v[1:6]
        v = v[0:4] + v[1:5]
        v = v[:, 0:5] + v[:, 1:6]
        v = v[:, 0:4] + v[:, 1:5]
        return (1.0 / 256.0) * (later(v, pos) + 2.0 * v + earlier(v, pos))

    j11, j22, j33 = smoothed(gi * gi), smoothed(gx * gx), smoothed(gt * gt)
    j12, j13, j23 = smoothed(gi * gx), smoothed(gi * gt), smoothed(gx * gt)
    trace = j11 + j22 + j33
    minors = j11 * j22 - j12 * j12 + j11 * j33 - j13 * j13 + j22 * j33 - j23 * j23
    coherence = 1.0 - 3.0 * minors / (trace * trace + epsilon)
    gi, gx = gi[1:5, 1:5], gx[1:5, 1:5]
    inside = e[2:6, 2:6]
    second = e[3:7, 2:6] + e[1:5, 2:6] + e[2:6, 3:7] + e[2:6, 1:5] - 4.0 * inside
    root = lax.rsqrt(1.0 + 0.25 * (gi * gi + gx * gx))
    curvature = second * (root * root * root)
    for r in range(rows):
        coh_ref[0, r] = jnp.where(r < width, coherence[r], 0.0).reshape((cols, SUB * LANE))
        coh_ref[1, r] = jnp.where(r < width, curvature[r], 0.0).reshape((cols, SUB * LANE))
    drain(*one)
    drain(*two)


def on_device(survey, conduct, widths):
    _, rows, cols, samples = survey.shape
    traces = jax.ShapeDtypeStruct((2, rows, cols, samples), jnp.float32)
    vmem = pl.BlockSpec(memory_space=pltpu.VMEM)
    hbm = pl.BlockSpec(memory_space=pl.ANY)
    buffer = lambda n: pltpu.VMEM((n, SUB, LANE), jnp.float32)
    both = pl.pallas_call(
        kernel,
        out_shape=traces,
        in_specs=[pl.BlockSpec(memory_space=pltpu.SMEM), hbm, hbm],
        out_specs=vmem,
        scratch_shapes=[
            pltpu.VMEM((rows, cols, samples), jnp.float32),
            pltpu.VMEM((3, rows, cols, samples), jnp.bfloat16),
            buffer(FIRST_LEN),
            buffer(FIRST_LEN),
            buffer(SECOND_LEN),
            buffer(SECOND_LEN),
            pltpu.SemaphoreType.DMA((2,)),
            pltpu.SemaphoreType.DMA((8,)),
            pltpu.SemaphoreType.DMA((8,)),
            pltpu.SemaphoreType.DMA((8,)),
            pltpu.SemaphoreType.DMA((8,)),
        ],
        compiler_params=pltpu.CompilerParams(
            collective_id=0, has_side_effects=True, vmem_limit_bytes=55000 * 1024
        ),
    )(widths.T, survey, conduct)
    return both[0:1], both[1:2]


def solution(mesh):
    placed = (
        P(None, "inline", "xline", None),
        P(None, None, "inline", "xline", None),
        P(None, "inline"),
    )
    return jax.shard_map(
        on_device,
        mesh=mesh,
        in_specs=placed,
        out_specs=(P("segment", "inline", "xline", None), P("segment", "inline", "xline", None)),
        check_vma=False,
    )
```
